512 devices in a mesh: gx: 32 (over x_lo, z), gy: 16 (over y, x_hi, core).
Axes of the slice: x: 4 (x_hi: 2, x_lo: 2; x = x_hi * 2 + x_lo), y: 4, z: 16, core: 2. Of those that a mesh axis runs over, the one named last changes fastest.
Arguments:
- impedance: bfloat16 [32, 16, 1024, 1024], P('gx', 'gy'), may hold values from -0.1875 to 0.1875
- rebuild_map: bfloat16 [32, 16, 256, 1024], P('gx', 'gy'), may hold values from -0.1875 to 0.1875
- left_trace: bfloat16 [32, 16, 512, 512], P('gx', 'gy'), may hold values from -6 to 6
- lower_trace: bfloat16 [32, 16, 512, 512], P('gx', 'gy'), may hold values from -6 to 6
- cell_kind: int32 [512, 256], P('gx', 'gy'), may hold values from 0 to 15
- kind_wavenum: float32 [16], replicated, may hold values from 0.5 to 3
Outputs:
- right_trace: bfloat16 [32, 16, 512, 512], P('gx', 'gy')
- upper_trace: bfloat16 [32, 16, 512, 512], P('gx', 'gy')
- residual: float32 [512, 256, 512], P('gx', 'gy')
The draws below stay inside these ranges and needn't reach their ends.
All inputs are finite; a program needn't handle non-finite values.
Results may differ from the reference program's by a relative error of at most 0.0064.
Values may be sent and summed in bfloat16 or wider, within the bound.
A program may use at most 64 MiB of HBM per device.

```python
import math
import jax
import jax.numpy as jnp
from jax import lax

TRACE = 512
SRC = 512
CX = 16
CY = 16
STEPS = 4
KINDS = 16
NX = 512
NY = 256
N_GX = 32
N_GY = 16


def with_ends(array, own_key, low, top_value):
    longest = array.shape.index(max(array.shape))
    spots = []
    for shift in (0, 1):
        where = [jax.random.randint(jax.random.fold_in(own_key, axis), (), 0, length) for axis, length in enumerate(array.shape)]
        where[longest] = (where[longest] + shift) % array.shape[longest]
        spots.append(tuple(where))
    return array.at[spots[0]].set(low).at[spots[1]].set(top_value)


def block_scale(rng, dims, shards, smallest, largest):
    gain = 1.0
    for axis_at, blocks in shards:
        draws = jax.random.uniform(jax.random.fold_in(jax.random.fold_in(rng, 6), axis_at), (blocks,), jnp.float32, smallest / len(shards), largest / len(shards))
        gain = gain * jnp.repeat(jnp.exp(draws), dims[axis_at] // blocks).reshape((-1,) + (1,) * (len(dims) - 1 - axis_at))
    return gain


def noise(key, shape, deviation, bound, pieces=(), dtype=jnp.bfloat16):
    result = deviation * jax.random.normal(key, shape, jnp.float32)
    if pieces:
        result = result * block_scale(key, shape, pieces, -0.22, 0.18)
    return jnp.clip(result, -bound, bound).astype(dtype)


def setup_inputs(seed: int = 0) -> dict:
    streams_of = jax.random.split(jax.random.key(seed), 7)
    return {
        "impedance": noise(streams_of[0], (N_GX, N_GY, 2 * TRACE, 2 * TRACE), (2 * TRACE) ** -0.5, 0.1875, ((0, 32), (1, 16))),
        "rebuild_map": noise(streams_of[1], (N_GX, N_GY, CX * CY, 2 * TRACE), (2 * TRACE) ** -0.5, 0.1875, ((0, 32), (1, 16))),
        "left_trace": noise(streams_of[2], (N_GX, N_GY, TRACE, SRC), 1.0, 6.0, ((0, 32), (1, 16))),
        "lower_trace": noise(streams_of[3], (N_GX, N_GY, TRACE, SRC), 1.0, 6.0, ((0, 32), (1, 16))),
        "cell_kind": with_ends(jax.random.randint(streams_of[4], (NX, NY), 0, KINDS), jax.random.fold_in(streams_of[4], 1), 0, KINDS - 1).astype(jnp.int32),
        "kind_wavenum": jnp.clip(jnp.exp(jax.random.uniform(streams_of[5], (KINDS,), jnp.float32, math.log(0.5), math.log(3.0))), 0.5, 3.0),
    }


def advance_all(impedance, left_in, lower_in):
    def per_row(items):
        mapping, left_row, lower_row = items
        stacked = jnp.concatenate([left_row, lower_row], axis=1).astype(jnp.float32)
        outgoing = jnp.einsum("gij,gjs->gis", mapping.astype(jnp.float32), stacked, precision=lax.Precision.HIGHEST)
        return outgoing.astype(jnp.bfloat16)

    outgoing = lax.map(per_row, (impedance, left_in, lower_in))
    return outgoing[:, :, :TRACE], outgoing[:, :, TRACE:]


def rebuild_all(rebuild_map, left_in, lower_in):
    def per_row(items):
        mapping, left_row, lower_row = items
        stacked = jnp.concatenate([left_row, lower_row], axis=1).astype(jnp.float32)
        return jnp.einsum("gcj,gjs->gcs", mapping.astype(jnp.float32), stacked, precision=lax.Precision.HIGHEST)

    return lax.map(per_row, (rebuild_map, left_in, lower_in))


def reference(impedance, rebuild_map, left_trace, lower_trace, cell_kind, kind_wavenum):
    left_in, lower_in = left_trace, lower_trace
    right_out, upper_out = left_in, lower_in
    for sweep_step in range(STEPS):
        right_out, upper_out = advance_all(impedance, left_in, lower_in)
        if sweep_step + 1 < STEPS:
            left_in = jnp.concatenate([jnp.zeros_like(right_out[:1]), right_out[:-1]], axis=0)
            lower_in = jnp.concatenate([jnp.zeros_like(upper_out[:, :1]), upper_out[:, :-1]], axis=1)
    tiles = rebuild_all(rebuild_map, left_in, lower_in)
    volume = tiles.reshape(N_GX, N_GY, CX, CY, SRC).transpose(0, 2, 1, 3, 4).reshape(NX, NY, SRC)
    padded = jnp.pad(volume, ((1, 1), (1, 1), (0, 0)))
    beside = padded[2:, 1:-1] + padded[:-2, 1:-1] + padded[1:-1, 2:] + padded[1:-1, :-2]
    wavenum = kind_wavenum[cell_kind]
    residual = beside - 4.0 * volume + wavenum[:, :, None] * volume
    return right_out, upper_out, residual
```

```python
import functools

import jax
import jax.numpy as jnp
from jax import lax
from jax.experimental import pallas as pl
from jax.experimental.pallas import tpu as pltpu
from jax.sharding import PartitionSpec as P

MESH = pl.DeviceIdType.MESH
STEPS = 4
LANES = 128
BY_WAY = (0, 2)


def remote(src, dst, send_sem, recv_sem, device):
    return pltpu.make_async_remote_copy(
        src_ref=src, dst_ref=dst, send_sem=send_sem, recv_sem=recv_sem,
        device_id=device, device_id_type=MESH,
    )


def sweep(
    n_gx, n_gy,
    impedance, rebuild_map, left, lower, kinds_hbm, wavenum_hbm,
    right_out, upper_out, residual,
    amap, bmap, traces, outgoing, way, volume, factor, beside, edge_out, edge_in,
    cell_kind, kind_wavenum, load_sem, map_sem, right_send, right_recv, upper_send, upper_recv, way_send, way_recv, edge_send, edge_recv,
):
    gx, gy = lax.axis_index("gx"), lax.axis_index("gy")
    rows = left.shape[0]
    chunks = left.shape[1] // LANES
    cells = rebuild_map.shape[0]
    cx, cy = cell_kind.shape
    half, last_x, last_y = n_gx // 2, n_gx - 1, n_gy - 1
    behind, ahead = lax.rem(gx + last_x, n_gx), lax.rem(gx + 1, n_gx)
    below, above = lax.rem(gy + last_y, n_gy), lax.rem(gy + 1, n_gy)

    def map_load(k):
        part = pl.ds(k * rows, rows)
        return pltpu.make_async_copy(impedance.at[part, :], amap.at[part, :], map_sem.at[k])

    def rebuild_load():
        return pltpu.make_async_copy(rebuild_map, bmap, map_sem.at[2])

    def kinds_load():
        return pltpu.make_async_copy(kinds_hbm, cell_kind, map_sem.at[3])

    def wavenum_load():
        return pltpu.make_async_copy(wavenum_hbm, kind_wavenum, map_sem.at[4])

    def trace_load(side, c):
        source = (left, lower)[side]
        return pltpu.make_async_copy(
            source.at[:, pl.ds(c * LANES, LANES)], traces.at[0, c, pl.ds(side * rows, rows), :], load_sem.at[side, c]
        )

    barrier = pltpu.get_barrier_semaphore()
    for device in ((behind, gy), (ahead, gy), (gx, below), (gx, above)):
        pl.semaphore_signal(barrier, inc=1, device_id=device, device_id_type=MESH)

    @pl.when((gx == half - 1) | (gx == half))
    def _():
        pl.semaphore_signal(barrier, inc=1, device_id=(last_x, gy), device_id_type=MESH)

    @pl.when(gx == last_x)
    def _():
        pl.semaphore_signal(barrier, inc=1, device_id=(half - 1, gy), device_id_type=MESH)
        pl.semaphore_signal(barrier, inc=1, device_id=(half, gy), device_id_type=MESH)

    map_load(0).start()
    for side in (0, 1):
        trace_load(side, 0).start()
    map_load(1).start()
    for c in range(1, chunks):
        for side in (0, 1):
            trace_load(side, c).start()
    rebuild_load().start()
    kinds_load().start()
    wavenum_load().start()

    def to_right(s, c):
        return remote(
            outgoing.at[s, c, pl.ds(0, rows), :], traces.at[s + 1, c, pl.ds(0, rows), :],
            right_send.at[s, c], right_recv.at[s, c], (ahead, gy),
        )

    def to_way(s, c):
        return remote(
            outgoing.at[s, c, pl.ds(0, rows), :], way.at[s, c], right_send.at[s, c], way_recv.at[s, c], (last_x, gy)
        )

    def from_way(s, c):
        return remote(
            way.at[s, c], traces.at[s + 1, c, pl.ds(0, rows), :], way_send.at[s, c], right_recv.at[s, c], (half, gy)
        )

    def to_upper(s, c):
        return remote(
            outgoing.at[s, c, pl.ds(rows, rows), :], traces.at[s + 1, c, pl.ds(rows, rows), :],
            upper_send.at[s, c], upper_recv.at[s, c], (gx, above),
        )

    def is_way(c):
        found = c == BY_WAY[0]
        for k in BY_WAY[1:]:
            found = found | (c == k)
        return found

    def send_right(s, c):
        by_way = (gx == half - 1) & is_way(c)

        @pl.when((gx < last_x) & jnp.logical_not(by_way))
        def _():
            to_right(s, c).start()

        @pl.when(by_way)
        def _():
            to_way(s, c).start()

    def arrived(s, c):
        @pl.when(gx > 0)
        def _():
            to_right(s, c).wait_recv()

        @pl.when((gx == last_x) & is_way(c))
        def _():
            to_way(s, c).wait_recv()
            from_way(s, c).start()

        @pl.when(gy > 0)
        def _():
            to_upper(s, c).wait_recv()

    def part(k, s, c):
        return jnp.dot(
            amap[pl.ds(k * rows, rows), :], traces[s, c], preferred_element_type=jnp.float32
        ).astype(jnp.bfloat16)

    def send_upper(s, c):
        @pl.when(gy < last_y)
        def _():
            to_upper(s, c).start()

    def advance(s, c):
        outgoing[s, c, pl.ds(0, rows), :] = part(0, s, c)
        send_right(s, c)
        outgoing[s, c, pl.ds(rows, rows), :] = part(1, s, c)
        send_upper(s, c)

    map_load(0).wait()
    for side in (0, 1):
        trace_load(side, 0).wait()
    outgoing[0, 0, pl.ds(0, rows), :] = part(0, 0, 0)
    greeted = jnp.where(gx == last_x, 6, jnp.where((gx == half - 1) | (gx == half), 5, 4))
    pl.semaphore_wait(barrier, greeted)
    send_right(0, 0)
    map_load(1).wait()
    outgoing[0, 0, pl.ds(rows, rows), :] = part(1, 0, 0)
    send_upper(0, 0)

    @pl.loop(1, chunks)
    def _(c):
        trace_load(0, c).wait()
        trace_load(1, c).wait()
        advance(0, c)

    def clear(side):
        @pl.loop(1, STEPS)
        def _(s):
            @pl.loop(0, chunks)
            def _(c):
                traces[s, c, pl.ds(side * rows, rows), :] = jnp.zeros((rows, LANES), traces.dtype)

    def clear_edge(k):
        edge_in[k] = jnp.zeros(edge_in.shape[1:], edge_in.dtype)

    @pl.when(gx == 0)
    def _():
        clear(0)
        clear_edge(0)

    @pl.when(gx == last_x)
    def _():
        clear_edge(1)

    @pl.when(gy == 0)
    def _():
        clear(1)
        clear_edge(2)

    @pl.when(gy == last_y)
    def _():
        clear_edge(3)

    kinds_load().wait()
    wavenum_load().wait()

    @pl.loop(0, cx)
    def _(a):
        @pl.loop(0, cy)
        def _(b):
            factor[pl.ds(a * cy + b, 1), :] = jnp.full((1, LANES), kind_wavenum[cell_kind[a, b]] - 4.0, jnp.float32)

    @pl.loop(1, STEPS - 1)
    def _(s):
        @pl.loop(0, chunks)
        def _(c):
            arrived(s - 1, c)
            advance(s, c)

    rebuild_load().wait()
    reach = (
        (gx > 0, gx < last_x, (ahead, gy)),
        (gx < last_x, gx > 0, (behind, gy)),
        (gy > 0, gy < last_y, (gx, above)),
        (gy < last_y, gy > 0, (gx, below)),
    )

    def edge_copy(k, c):
        return remote(
            edge_out.at[k, c], edge_in.at[k, c], edge_send.at[k, c], edge_recv.at[k, c], reach[k][2]
        )

    def rebuild(c):
        volume[c] = jnp.dot(bmap[...], traces[STEPS - 1, c], preferred_element_type=jnp.float32)
        edge_out[0, c] = volume[c, pl.ds(cells - cy, cy), :].astype(edge_out.dtype)
        edge_out[1, c] = volume[c, pl.ds(0, cy), :].astype(edge_out.dtype)
        edge_out[2, c] = volume[c, pl.ds(cy - 1, cx, stride=cy), :].astype(edge_out.dtype)
        edge_out[3, c] = volume[c, pl.ds(0, cx, stride=cy), :].astype(edge_out.dtype)
        for k in range(4):
            @pl.when(reach[k][1])
            def _(k=k):
                edge_copy(k, c).start()

    def finish(c):
        for k in range(4):
            @pl.when(reach[k][0])
            def _(k=k):
                edge_copy(k, c).wait_recv()
        cell = volume[c]
        beside[0] = pltpu.roll(cell, 1, 0)
        beside[1] = pltpu.roll(cell, cells - 1, 0)
        beside[0, pl.ds(0, cx, stride=cy), :] = edge_in[2, c].astype(jnp.float32)
        beside[1, pl.ds(cy - 1, cx, stride=cy), :] = edge_in[3, c].astype(jnp.float32)
        along_x = jnp.concatenate([edge_in[0, c].astype(jnp.float32), cell[: cells - cy]], axis=0) + jnp.concatenate(
            [cell[cy:], edge_in[1, c].astype(jnp.float32)], axis=0
        )
        residual[:, pl.ds(pl.multiple_of(c * LANES, LANES), LANES)] = (
            along_x + beside[0] + beside[1] + factor[...] * cell
        )

    @pl.loop(0, chunks)
    def _(c):
        arrived(STEPS - 2, c)
        rebuild(c)
        lanes = pl.ds(pl.multiple_of(c * LANES, LANES), LANES)
        right_out[:, lanes] = part(0, STEPS - 1, c)
        upper_out[:, lanes] = part(1, STEPS - 1, c)

        @pl.when(c > 0)
        def _():
            finish(c - 1)

    finish(chunks - 1)

    @pl.loop(0, STEPS - 1)
    def _(s):
        @pl.loop(0, chunks)
        def _(c):
            @pl.when(gx < last_x)
            def _():
                to_right(s, c).wait_send()

            @pl.when((gx == last_x) & is_way(c))
            def _():
                from_way(s, c).wait_send()

            @pl.when(gy < last_y)
            def _():
                to_upper(s, c).wait_send()

    @pl.loop(0, chunks)
    def _(c):
        for k in range(4):
            @pl.when(reach[k][1])
            def _(k=k):
                edge_copy(k, c).wait_send()


def per_device(n_gx, n_gy, impedance, rebuild_map, left_trace, lower_trace, cell_kind, kind_wavenum):
    rows, sources = left_trace.shape[2:]
    cells = rebuild_map.shape[2]
    cx, cy = cell_kind.shape
    chunks = sources // LANES
    bf16, f32 = jnp.bfloat16, jnp.float32
    pair = lambda *shape: [pltpu.SemaphoreType.DMA(shape)] * 2
    right, upper, residual = pl.pallas_call(
        functools.partial(sweep, n_gx, n_gy),
        out_shape=(
            pltpu.VMEM((rows, sources), bf16),
            pltpu.VMEM((rows, sources), bf16),
            pltpu.VMEM((cells, sources), f32),
        ),
        in_specs=[pl.BlockSpec(memory_space=pltpu.HBM)] * 6,
        out_specs=[pl.BlockSpec(memory_space=pltpu.VMEM)] * 3,
        scratch_shapes=[
            pltpu.VMEM((2 * rows, 2 * rows), bf16),
            pltpu.VMEM((cells, 2 * rows), bf16),
            pltpu.VMEM((STEPS, chunks, 2 * rows, LANES), bf16),
            pltpu.VMEM((STEPS - 1, chunks, 2 * rows, LANES), bf16),
            pltpu.VMEM((STEPS - 1, chunks, rows, LANES), bf16),
            pltpu.VMEM((chunks, cells, LANES), f32),
            pltpu.VMEM((cells, LANES), f32),
            pltpu.VMEM((2, cells, LANES), f32),
            pltpu.VMEM((4, chunks, cy, LANES), bf16),
            pltpu.VMEM((4, chunks, cy, LANES), bf16),
            pltpu.SMEM((cx, cy), jnp.int32),
            pltpu.SMEM(kind_wavenum.shape, f32),
            pltpu.SemaphoreType.DMA((2, chunks)),
            pltpu.SemaphoreType.DMA((5,)),
            *pair(STEPS - 1, chunks),
            *pair(STEPS - 1, chunks),
            *pair(STEPS - 1, chunks),
            *pair(4, chunks),
        ],
        compiler_params=pltpu.CompilerParams(
            collective_id=0, has_side_effects=True, vmem_limit_bytes=40 * 2**20
        ),
        cost_estimate=pl.CostEstimate(flops=4_600_000_000, bytes_accessed=5_300_000, transcendentals=0),
        name="sweep",
    )(*[
        pltpu.with_memory_space_constraint(array, pltpu.HBM)
        for array in (impedance[0, 0], rebuild_map[0, 0], left_trace[0, 0], lower_trace[0, 0], cell_kind, kind_wavenum)
    ])
    return right[None, None], upper[None, None], residual.reshape(cx, cy, sources)


def solution(mesh):
    return jax.shard_map(
        functools.partial(per_device, mesh.shape["gx"], mesh.shape["gy"]),
        mesh=mesh,
        in_specs=(
            P("gx", "gy", None, None),
            P("gx", "gy", None, None),
            P("gx", "gy", None, None),
            P("gx", "gy", None, None),
            P("gx", "gy"),
            P(),
        ),
        out_specs=(P("gx", "gy", None, None), P("gx", "gy", None, None), P("gx", "gy", None)),
        check_vma=False,
    )
```

```python
import functools

import jax
import jax.numpy as jnp
from jax import lax
from jax.experimental import pallas as pl
from jax.experimental.pallas import tpu as pltpu
from jax.sharding import PartitionSpec as P

MESH = pl.DeviceIdType.MESH
STEPS = 4
LANES = 128

def remote(src, dst, send_sem, recv_sem, device):
    return pltpu.make_async_remote_copy(
        src_ref=src, dst_ref=dst, send_sem=send_sem, recv_sem=recv_sem,
        device_id=device, device_id_type=MESH,
    )


def sweep(
    n_gx, n_gy,
    impedance, rebuild_map, left, lower, kinds_hbm, wavenum_hbm,
    right_out, upper_out, residual,
    amap, bmap, traces, outgoing, way, emap, factor, beside, edge_out, edge_in,
    cell_kind, kind_wavenum, load_sem, map_sem, right_send, right_recv, upper_send, upper_recv, way_send, way_recv, edge_send, edge_recv,
):
    gx, gy = lax.axis_index("gx"), lax.axis_index("gy")
    rows = left.shape[0]
    chunks = left.shape[1] // LANES
    cells = rebuild_map.shape[0]
    cx, cy = cell_kind.shape
    half, last_x, last_y = n_gx // 2, n_gx - 1, n_gy - 1
    behind, ahead = lax.rem(gx + last_x, n_gx), lax.rem(gx + 1, n_gx)
    below, above = lax.rem(gy + last_y, n_gy), lax.rem(gy + 1, n_gy)

    quarter = rows // 2

    def map_load(k):
        part = pl.ds(k * quarter, quarter)
        return pltpu.make_async_copy(impedance.at[part, :], amap.at[part, :], map_sem.at[k])

    def rebuild_load():
        return pltpu.make_async_copy(rebuild_map, bmap, map_sem.at[6])

    def kinds_load():
        return pltpu.make_async_copy(kinds_hbm, cell_kind, map_sem.at[4])

    def wavenum_load():
        return pltpu.make_async_copy(wavenum_hbm, kind_wavenum, map_sem.at[5])

    def trace_load(side, c):
        source = (left, lower)[side]
        return pltpu.make_async_copy(
            source.at[:, pl.ds(c * LANES, LANES)], traces.at[0, c, pl.ds(side * rows, rows), :], load_sem.at[side, c]
        )

    for side in (0, 1):
        trace_load(side, 0).start()
    for k in range(4):
        map_load(k).start()
    for c in range(1, chunks):
        for side in (0, 1):
            trace_load(side, c).start()
    rebuild_load().start()
    kinds_load().start()
    wavenum_load().start()

    barrier = pltpu.get_barrier_semaphore()
    senders = (
        (gx > 0, (behind, gy)),
        (gy > 0, (gx, below)),
        (gx == last_x, (half - 1, gy)),
        (gx == half, (last_x, gy)),
    )
    for present, device in senders:
        @pl.when(present)
        def _(device=device):
            pl.semaphore_signal(barrier, inc=1, device_id=device, device_id_type=MESH)

    greeted = 0
    for present in (gx < last_x, gy < last_y, gx == half - 1, gx == last_x):
        greeted = greeted + jnp.where(present, 1, 0)

    def to_right(s, c):
        return remote(
            outgoing.at[s, c, pl.ds(0, rows), :], traces.at[s + 1, c, pl.ds(0, rows), :],
            right_send.at[s, c], right_recv.at[s, c], (ahead, gy),
        )

    def to_way(s, c):
        return remote(
            outgoing.at[s, c, pl.ds(0, rows), :], way.at[s, c], right_send.at[s, c], way_recv.at[s, c], (last_x, gy)
        )

    def from_way(s, c):
        return remote(
            way.at[s, c], traces.at[s + 1, c, pl.ds(0, rows), :], way_send.at[s, c], right_recv.at[s, c], (half, gy)
        )

    def to_upper(s, c):
        return remote(
            outgoing.at[s, c, pl.ds(rows, rows), :], traces.at[s + 1, c, pl.ds(rows, rows), :],
            upper_send.at[s, c], upper_recv.at[s, c], (gx, above),
        )

    def is_way(s, c):
        return ((s == 0) & (c >= chunks // 2)) | ((s == 1) & (lax.rem(c, 2) == 0))

    def send_right(s, c):
        by_way = (gx == half - 1) & is_way(s, c)

        @pl.when((gx < last_x) & jnp.logical_not(by_way))
        def _():
            to_right(s, c).start()

        @pl.when(by_way)
        def _():
            to_way(s, c).start()

    def arrived(s, c):
        @pl.when(gx > 0)
        def _():
            to_right(s, c).wait_recv()

        @pl.when(gy > 0)
        def _():
            to_upper(s, c).wait_recv()

    def relay(s, c):
        @pl.when((gx == last_x) & is_way(s, c))
        def _():
            to_way(s, c).wait_recv()
            from_way(s, c).start()

    def multiply(s, c):
        return jnp.dot(amap[...], traces[s, c], preferred_element_type=jnp.float32).astype(jnp.bfloat16)

    def send_upper(s, c):
        @pl.when(gy < last_y)
        def _():
            to_upper(s, c).start()

    def advance(s, c):
        outgoing[s, c] = multiply(s, c)
        send_right(s, c)
        send_upper(s, c)

    for side in (0, 1):
        trace_load(side, 0).wait()
    for k in range(4):
        map_load(k).wait()
        part = pl.ds(k * quarter, quarter)
        outgoing[0, 0, part, :] = jnp.dot(
            amap[part, :], traces[0, 0], preferred_element_type=jnp.float32
        ).astype(jnp.bfloat16)
        if k == 1:
            pl.semaphore_wait(barrier, greeted)
            send_right(0, 0)
    send_upper(0, 0)

    @pl.loop(1, chunks)
    def _(c):
        trace_load(0, c).wait()
        trace_load(1, c).wait()
        advance(0, c)

    def clear(side):
        @pl.loop(1, STEPS)
        def _(s):
            @pl.loop(0, chunks)
            def _(c):
                traces[s, c, pl.ds(side * rows, rows), :] = jnp.zeros((rows, LANES), traces.dtype)

    def clear_edge(k):
        edge_in[:, pl.ds(k * cy, cy), :] = jnp.zeros((chunks, cy, LANES), edge_in.dtype)

    @pl.when(gx == 0)
    def _():
        clear(0)
        clear_edge(0)

    @pl.when(gx == last_x)
    def _():
        clear_edge(1)

    @pl.when(gy == 0)
    def _():
        clear(1)
        clear_edge(2)

    @pl.when(gy == last_y)
    def _():
        clear_edge(3)

    rebuild_load().wait()
    row = lax.broadcasted_iota(jnp.int32, (4 * cy, cells), 0)
    side, along = lax.div(row, cy), lax.rem(row, cy)
    chosen = jnp.where(
        side == 0, cells - cy + along, jnp.where(side == 1, along, jnp.where(side == 2, along * cy + cy - 1, along * cy))
    )
    chosen = lax.broadcasted_iota(jnp.int32, (4 * cy, cells), 1) == chosen
    emap[...] = jnp.dot(
        jnp.where(chosen, 1.0, 0.0).astype(jnp.bfloat16), bmap[...], preferred_element_type=jnp.float32
    ).astype(jnp.bfloat16)

    @pl.loop(1, STEPS - 1)
    def _(s):
        @pl.loop(0, chunks)
        def _(c):
            arrived(s - 1, c)
            advance(s, c)

            @pl.when((s == 1) & (c < chunks // 2))
            def _():
                relay(0, c + chunks // 2)

            @pl.when((s == 1) & (c == chunks // 2))
            def _():
                relay(1, 0)

            @pl.when((s == 2) & (c == 0))
            def _():
                relay(1, chunks // 2)

    reach = (
        (gx > 0, gx < last_x, (ahead, gy)),
        (gx < last_x, gx > 0, (behind, gy)),
        (gy > 0, gy < last_y, (gx, above)),
        (gy < last_y, gy > 0, (gx, below)),
    )

    def edge_copy(k, c):
        part = pl.ds(k * cy, cy)
        return remote(
            edge_out.at[c, part, :], edge_in.at[c, part, :], edge_send.at[k, c], edge_recv.at[k, c], reach[k][2]
        )

    def send_edges(c):
        edge_out[c] = jnp.dot(
            emap[...], traces[STEPS - 1, c], preferred_element_type=jnp.float32
        ).astype(edge_out.dtype)
        for k in range(4):
            @pl.when(reach[k][1])
            def _(k=k):
                edge_copy(k, c).start()

    first, last = pl.ds(0, cx, stride=cy), pl.ds(cy - 1, cx, stride=cy)

    def rebuild(c):
        cell = jnp.dot(bmap[...], traces[STEPS - 1, c], preferred_element_type=jnp.float32)
        none = jnp.zeros((cy, LANES), jnp.float32)
        beside[0] = pltpu.roll(cell, 1, 0)
        beside[1] = pltpu.roll(cell, cells - 1, 0)
        beside[0, first, :] = none
        beside[1, last, :] = none
        along_x = jnp.concatenate([none, cell[: cells - cy]], axis=0) + jnp.concatenate([cell[cy:], none], axis=0)
        residual[c] = along_x + beside[0] + beside[1] + factor[...] * cell

    def finish(c):
        for k in range(4):
            @pl.when(reach[k][0])
            def _(k=k):
                edge_copy(k, c).wait_recv()
        for k, part in enumerate((pl.ds(0, cy), pl.ds(cells - cy, cy), first, last)):
            residual[c, part, :] += edge_in[c, pl.ds(k * cy, cy), :].astype(jnp.float32)

    @pl.loop(0, chunks)
    def _(c):
        arrived(STEPS - 2, c)
        send_edges(c)

        @pl.when(c == 0)
        def _():
            kinds_load().wait()
            wavenum_load().wait()

            @pl.loop(0, cx)
            def _(a):
                for b in range(cy):
                    factor[pl.ds(a * cy + b, 1), :] = jnp.full(
                        (1, LANES), kind_wavenum[cell_kind[a, b]] - 4.0, jnp.float32
                    )

        rebuild(c)
        lanes = pl.ds(pl.multiple_of(c * LANES, LANES), LANES)
        leaving = multiply(STEPS - 1, c)
        right_out[:, lanes] = leaving[:rows]
        upper_out[:, lanes] = leaving[rows:]

        @pl.when(c > 0)
        def _():
            finish(c - 1)

    finish(chunks - 1)

    @pl.loop(0, STEPS - 1)
    def _(s):
        @pl.loop(0, chunks)
        def _(c):
            @pl.when(gx < last_x)
            def _():
                to_right(s, c).wait_send()

            @pl.when((gx == last_x) & is_way(s, c))
            def _():
                from_way(s, c).wait_send()

            @pl.when(gy < last_y)
            def _():
                to_upper(s, c).wait_send()

    @pl.loop(0, chunks)
    def _(c):
        for k in range(4):
            @pl.when(reach[k][1])
            def _(k=k):
                edge_copy(k, c).wait_send()


def flush(right, upper, residual, right_out, upper_out, residual_out, sem):
    copies = [
        pltpu.make_async_copy(right, right_out, sem.at[0]),
        pltpu.make_async_copy(upper, upper_out, sem.at[1]),
    ]
    for c in range(residual.shape[0]):
        lanes = pl.ds(c * LANES, LANES)
        copies.append(pltpu.make_async_copy(residual.at[c], residual_out.at[:, lanes], sem.at[2 + c]))
    for copy in copies:
        copy.start()
    for copy in copies:
        copy.wait()


def per_device(n_gx, n_gy, impedance, rebuild_map, left_trace, lower_trace, cell_kind, kind_wavenum):
    rows, sources = left_trace.shape[2:]
    cells = rebuild_map.shape[2]
    cx, cy = cell_kind.shape
    chunks = sources // LANES
    bf16, f32 = jnp.bfloat16, jnp.float32
    pair = lambda *shape: [pltpu.SemaphoreType.DMA(shape)] * 2
    right, upper, residual = pl.pallas_call(
        functools.partial(sweep, n_gx, n_gy),
        out_shape=(
            pltpu.VMEM((rows, sources), bf16),
            pltpu.VMEM((rows, sources), bf16),
            pltpu.VMEM((chunks, cells, LANES), f32),
        ),
        in_specs=[pl.BlockSpec(memory_space=pltpu.HBM)] * 6,
        out_specs=[pl.BlockSpec(memory_space=pltpu.VMEM)] * 3,
        scratch_shapes=[
            pltpu.VMEM((2 * rows, 2 * rows), bf16),
            pltpu.VMEM((cells, 2 * rows), bf16),
            pltpu.VMEM((STEPS, chunks, 2 * rows, LANES), bf16),
            pltpu.VMEM((STEPS - 1, chunks, 2 * rows, LANES), bf16),
            pltpu.VMEM((STEPS - 1, chunks, rows, LANES), bf16),
            pltpu.VMEM((4 * cy, 2 * rows), bf16),
            pltpu.VMEM((cells, LANES), f32),
            pltpu.VMEM((2, cells, LANES), f32),
            pltpu.VMEM((chunks, 4 * cy, LANES), bf16),
            pltpu.VMEM((chunks, 4 * cy, LANES), bf16),
            pltpu.SMEM((cx, cy), jnp.int32),
            pltpu.SMEM(kind_wavenum.shape, f32),
            pltpu.SemaphoreType.DMA((2, chunks)),
            pltpu.SemaphoreType.DMA((7,)),
            *pair(STEPS - 1, chunks),
            *pair(STEPS - 1, chunks),
            *pair(STEPS - 1, chunks),
            *pair(4, chunks),
        ],
        compiler_params=pltpu.CompilerParams(
            collective_id=0, has_side_effects=True, vmem_limit_bytes=40 * 2**20
        ),
        cost_estimate=pl.CostEstimate(flops=4_600_000_000, bytes_accessed=5_300_000, transcendentals=0),
        name="sweep",
    )(*[
        pltpu.with_memory_space_constraint(array, pltpu.HBM)
        for array in (impedance[0, 0], rebuild_map[0, 0], left_trace[0, 0], lower_trace[0, 0], cell_kind, kind_wavenum)
    ])
    right, upper, residual = pl.pallas_call(
        flush,
        out_shape=[jax.ShapeDtypeStruct((rows, sources), bf16)] * 2 + [jax.ShapeDtypeStruct((cells, sources), f32)],
        in_specs=[pl.BlockSpec(memory_space=pltpu.VMEM)] * 3,
        out_specs=[pl.BlockSpec(memory_space=pl.ANY)] * 3,
        scratch_shapes=[pltpu.SemaphoreType.DMA((2 + chunks,))],
        name="flush",
    )(*[pltpu.with_memory_space_constraint(array, pltpu.VMEM) for array in (right, upper, residual)])
    return right[None, None], upper[None, None], residual.reshape(cx, cy, sources)


def solution(mesh):
    return jax.shard_map(
        functools.partial(per_device, mesh.shape["gx"], mesh.shape["gy"]),
        mesh=mesh,
        in_specs=(
            P("gx", "gy", None, None),
            P("gx", "gy", None, None),
            P("gx", "gy", None, None),
            P("gx", "gy", None, None),
            P("gx", "gy"),
            P(),
        ),
        out_specs=(P("gx", "gy", None, None), P("gx", "gy", None, None), P("gx", "gy", None)),
        check_vma=False,
    )
```

```python
import functools

import jax
import jax.numpy as jnp
from jax import lax
from jax.experimental import pallas as pl
from jax.experimental.pallas import tpu as pltpu
from jax.sharding import PartitionSpec as P

MESH = pl.DeviceIdType.MESH
STEPS = 4
LANES = 128

def remote(src, dst, send_sem, recv_sem, device):
    return pltpu.make_async_remote_copy(
        src_ref=src, dst_ref=dst, send_sem=send_sem, recv_sem=recv_sem,
        device_id=device, device_id_type=MESH,
    )


def sweep(
    n_gx, n_gy,
    impedance, rebuild_map, left, lower, kinds_hbm, wavenum_hbm,
    right_out, upper_out, residual,
    amap, bmap, traces, outgoing, way, emap, factor, beside, edge_out, edge_in,
    lent, composed, early_out, early_in, joined,
    cell_kind, kind_wavenum, load_sem, map_sem, right_send, right_recv, upper_send, upper_recv, way_send, way_recv, edge_send, edge_recv,
    lend_send, lend_recv, early_send, early_recv,
):
    gx, gy = lax.axis_index("gx"), lax.axis_index("gy")
    rows = left.shape[0]
    chunks = left.shape[1] // LANES
    cells = rebuild_map.shape[0]
    cx, cy = cell_kind.shape
    half, last_x, last_y = n_gx // 2, n_gx - 1, n_gy - 1
    behind, ahead = lax.rem(gx + last_x, n_gx), lax.rem(gx + 1, n_gx)
    below, above = lax.rem(gy + last_y, n_gy), lax.rem(gy + 1, n_gy)

    quarter = rows // 2

    def map_load(k):
        part = pl.ds(k * quarter, quarter)
        return pltpu.make_async_copy(impedance.at[part, :], amap.at[part, :], map_sem.at[k])

    def rebuild_load():
        return pltpu.make_async_copy(rebuild_map, bmap, map_sem.at[6])

    def kinds_load():
        return pltpu.make_async_copy(kinds_hbm, cell_kind, map_sem.at[4])

    def wavenum_load():
        return pltpu.make_async_copy(wavenum_hbm, kind_wavenum, map_sem.at[5])

    def trace_load(side, c):
        source = (left, lower)[side]
        return pltpu.make_async_copy(
            source.at[:, pl.ds(c * LANES, LANES)], traces.at[0, c, pl.ds(side * rows, rows), :], load_sem.at[side, c]
        )

    for side in (0, 1):
        trace_load(side, 0).start()
    for k in range(4):
        map_load(k).start()
    for c in range(1, chunks):
        for side in (0, 1):
            trace_load(side, c).start()
    rebuild_load().start()
    kinds_load().start()
    wavenum_load().start()

    barrier = pltpu.get_barrier_semaphore()
    senders = (
        (gx > 0, (behind, gy)),
        (gy > 0, (gx, below)),
        (gx == last_x, (half - 1, gy)),
        (gx == half, (last_x, gy)),
        ((gx == half) & (lax.rem(gy, 2) == 0) & (gy > 0), (0, below)),
        ((gx == 0) & (lax.rem(gy, 2) == 0) & (gy > 0), (half, gy)),
    )
    for present, device in senders:
        @pl.when(present)
        def _(device=device):
            pl.semaphore_signal(barrier, inc=1, device_id=device, device_id_type=MESH)

    greeted = 0
    for present in (
        gx < last_x, gy < last_y, gx == half - 1, gx == last_x,
        (gx == 0) & (lax.rem(gy, 2) == 1) & (gy < last_y),
        (gx == half) & (lax.rem(gy, 2) == 0) & (gy > 0),
    ):
        greeted = greeted + jnp.where(present, 1, 0)

    def to_right(s, c):
        return remote(
            outgoing.at[s, c, pl.ds(0, rows), :], traces.at[s + 1, c, pl.ds(0, rows), :],
            right_send.at[s, c], right_recv.at[s, c], (ahead, gy),
        )

    def to_way(s, c):
        return remote(
            outgoing.at[s, c, pl.ds(0, rows), :], way.at[s, c], right_send.at[s, c], way_recv.at[s, c], (last_x, gy)
        )

    def from_way(s, c):
        return remote(
            way.at[s, c], traces.at[s + 1, c, pl.ds(0, rows), :], way_send.at[s, c], right_recv.at[s, c], (half, gy)
        )

    def to_upper(s, c):
        return remote(
            outgoing.at[s, c, pl.ds(rows, rows), :], traces.at[s + 1, c, pl.ds(rows, rows), :],
            upper_send.at[s, c], upper_recv.at[s, c], (gx, above),
        )

    def is_way(s, c):
        return ((s == 0) & (c >= chunks // 2))

    def send_right(s, c):
        by_way = (gx == half - 1) & is_way(s, c)

        @pl.when((gx < last_x) & jnp.logical_not(by_way))
        def _():
            to_right(s, c).start()

        @pl.when(by_way)
        def _():
            to_way(s, c).start()

    def arrived(s, c):
        @pl.when(gx > 0)
        def _():
            to_right(s, c).wait_recv()

        @pl.when(gy > 0)
        def _():
            to_upper(s, c).wait_recv()

    def relay(s, c):
        @pl.when((gx == last_x) & is_way(s, c))
        def _():
            to_way(s, c).wait_recv()
            from_way(s, c).start()

    odd = lax.rem(gy, 2) == 1
    detour = (gx == 0) & odd & (gy < last_y)
    beside_me = (gx == half) & jnp.logical_not(odd) & (gy > 0)

    def to_beside(s, c):
        return remote(
            outgoing.at[s, c, pl.ds(rows, rows), :], way.at[s, c], upper_send.at[s, c], way_recv.at[s, c], (half, above)
        )

    def from_beside(s, c):
        return remote(
            way.at[s, c], traces.at[s + 1, c, pl.ds(rows, rows), :], way_send.at[s, c], upper_recv.at[s, c], (0, gy)
        )

    def beside_relay(s, c):
        @pl.when(beside_me)
        def _():
            to_beside(s, c).wait_recv()
            from_beside(s, c).start()

    def multiply(s, c):
        return jnp.dot(amap[...], traces[s, c], preferred_element_type=jnp.float32).astype(jnp.bfloat16)

    def send_upper(s, c):
        @pl.when((gy < last_y) & jnp.logical_not(detour))
        def _():
            to_upper(s, c).start()

        @pl.when(detour)
        def _():
            to_beside(s, c).start()

    def advance(s, c):
        outgoing[s, c] = multiply(s, c)
        send_right(s, c)
        send_upper(s, c)

    for side in (0, 1):
        trace_load(side, 0).wait()
    for k in range(4):
        map_load(k).wait()
        part = pl.ds(k * quarter, quarter)
        outgoing[0, 0, part, :] = jnp.dot(
            amap[part, :], traces[0, 0], preferred_element_type=jnp.float32
        ).astype(jnp.bfloat16)
        if k == 1:
            pl.semaphore_wait(barrier, greeted)
            send_right(0, 0)
    send_upper(0, 0)

    @pl.loop(1, chunks)
    def _(c):
        trace_load(0, c).wait()
        trace_load(1, c).wait()
        advance(0, c)

    @pl.loop(0, chunks)
    def _(c):
        beside_relay(0, c)

    def clear(side):
        @pl.loop(1, STEPS)
        def _(s):
            @pl.loop(0, chunks)
            def _(c):
                traces[s, c, pl.ds(side * rows, rows), :] = jnp.zeros((rows, LANES), traces.dtype)

    def clear_edge(k):
        edge_in[:, pl.ds(k * cy, cy), :] = jnp.zeros((chunks, cy, LANES), edge_in.dtype)

    @pl.when(gx == 0)
    def _():
        clear(0)
        clear_edge(0)

    @pl.when(gx == last_x)
    def _():
        clear_edge(1)

    @pl.when(gy == 0)
    def _():
        clear(1)
        clear_edge(2)

    @pl.when(gy == last_y)
    def _():
        clear_edge(3)

    rebuild_load().wait()
    row = lax.broadcasted_iota(jnp.int32, (4 * cy, cells), 0)
    side, along = lax.div(row, cy), lax.rem(row, cy)
    chosen = jnp.where(
        side == 0, cells - cy + along, jnp.where(side == 1, along, jnp.where(side == 2, along * cy + cy - 1, along * cy))
    )
    chosen = lax.broadcasted_iota(jnp.int32, (4 * cy, cells), 1) == chosen
    emap[...] = jnp.dot(
        jnp.where(chosen, 1.0, 0.0).astype(jnp.bfloat16), bmap[...], preferred_element_type=jnp.float32
    ).astype(jnp.bfloat16)

    from_left, from_lower = gx == half - 2, (gx == half - 1) & (gy < last_y)
    joins, joins_lower = gx == half - 1, (gx == half - 1) & (gy > 0)

    def lend(k):
        return remote(
            bmap.at[pl.ds(cells - cy, cy), pl.ds(k * rows, rows)], lent.at[k], lend_send.at[k], lend_recv.at[k],
            ((behind, gy), (gx, below))[k],
        )

    def early(k, c):
        return remote(
            early_out.at[c], early_in.at[k, c], early_send.at[c], early_recv.at[k, c], ((ahead, gy), (gx, above))[k]
        )

    def lend_rows():
        for k, present in enumerate((joins, joins_lower)):
            @pl.when(present)
            def _(k=k):
                lend(k).start()

    def compose():
        for k, present in enumerate((from_left, from_lower)):
            @pl.when(present)
            def _(k=k):
                lend(k).wait_recv()
                composed[...] = jnp.dot(
                    lent[k], amap[pl.ds(k * rows, rows), :], preferred_element_type=jnp.float32
                ).astype(composed.dtype)

    def send_early(c):
        @pl.when(from_left | from_lower)
        def _():
            early_out[c] = jnp.dot(
                composed[...], traces[STEPS - 2, c], preferred_element_type=jnp.float32
            ).astype(early_out.dtype)

        for k, present in enumerate((from_left, from_lower)):
            @pl.when(present)
            def _(k=k):
                early(k, c).start()

    @pl.when((gx == half - 1) & (gy == 0))
    def _():
        early_in[1] = jnp.zeros(early_in.shape[1:], early_in.dtype)

    @pl.loop(1, STEPS - 1)
    def _(s):
        @pl.loop(0, chunks)
        def _(c):
            arrived(s - 1, c)

            @pl.when((s == 1) & (c == 0))
            def _():
                lend_rows()

            @pl.when((s == 2) & (c == 0))
            def _():
                compose()

            @pl.when(s == 2)
            def _():
                send_early(c)

            advance(s, c)

            @pl.when((s == 1) & (c < chunks // 2))
            def _():
                relay(0, c + chunks // 2)

            beside_relay(s, c)


    reach = (
        (gx > 0, gx < last_x, (ahead, gy)),
        (gx < last_x, gx > 0, (behind, gy)),
        (gy > 0, gy < last_y, (gx, above)),
        (gy < last_y, gy > 0, (gx, below)),
    )

    def join_early():
        @pl.when(joins)
        def _():
            @pl.loop(0, chunks)
            def _(c):
                early(0, c).wait_recv()

                @pl.when(gy > 0)
                def _():
                    early(1, c).wait_recv()

                joined[c] = (early_in[0, c].astype(jnp.float32) + early_in[1, c].astype(jnp.float32)).astype(joined.dtype)
                remote(
                    joined.at[c], edge_in.at[c, pl.ds(0, cy), :], edge_send.at[0, c], edge_recv.at[0, c], (ahead, gy)
                ).start()

    def edge_copy(k, c):
        part = pl.ds(k * cy, cy)
        return remote(
            edge_out.at[c, part, :], edge_in.at[c, part, :], edge_send.at[k, c], edge_recv.at[k, c], reach[k][2]
        )

    def send_edges(c):
        edge_out[c] = jnp.dot(
            emap[...], traces[STEPS - 1, c], preferred_element_type=jnp.float32
        ).astype(edge_out.dtype)
        for k in range(4):
            @pl.when(reach[k][1] & jnp.logical_not(joins) if k == 0 else reach[k][1])
            def _(k=k):
                edge_copy(k, c).start()

    first, last = pl.ds(0, cx, stride=cy), pl.ds(cy - 1, cx, stride=cy)

    def rebuild(c):
        cell = jnp.dot(bmap[...], traces[STEPS - 1, c], preferred_element_type=jnp.float32)
        none = jnp.zeros((cy, LANES), jnp.float32)
        beside[0] = pltpu.roll(cell, 1, 0)
        beside[1] = pltpu.roll(cell, cells - 1, 0)
        beside[0, first, :] = none
        beside[1, last, :] = none
        along_x = jnp.concatenate([none, cell[: cells - cy]], axis=0) + jnp.concatenate([cell[cy:], none], axis=0)
        residual[c] = along_x + beside[0] + beside[1] + factor[...] * cell

    def finish(c):
        for k in range(4):
            @pl.when(reach[k][0])
            def _(k=k):
                edge_copy(k, c).wait_recv()
        for k, part in enumerate((pl.ds(0, cy), pl.ds(cells - cy, cy), first, last)):
            residual[c, part, :] += edge_in[c, pl.ds(k * cy, cy), :].astype(jnp.float32)

    @pl.loop(0, chunks)
    def _(c):
        arrived(STEPS - 2, c)
        send_edges(c)

        @pl.when(c == 0)
        def _():
            join_early()
            kinds_load().wait()
            wavenum_load().wait()

            @pl.loop(0, cx)
            def _(a):
                for b in range(cy):
                    factor[pl.ds(a * cy + b, 1), :] = jnp.full(
                        (1, LANES), kind_wavenum[cell_kind[a, b]] - 4.0, jnp.float32
                    )

        rebuild(c)
        lanes = pl.ds(pl.multiple_of(c * LANES, LANES), LANES)
        leaving = multiply(STEPS - 1, c)
        right_out[:, lanes] = leaving[:rows]
        upper_out[:, lanes] = leaving[rows:]

    @pl.loop(0, chunks)
    def _(c):
        finish(c)

    @pl.loop(0, STEPS - 1)
    def _(s):
        @pl.loop(0, chunks)
        def _(c):
            @pl.when(gx < last_x)
            def _():
                to_right(s, c).wait_send()

            @pl.when((gx == last_x) & is_way(s, c))
            def _():
                from_way(s, c).wait_send()

            @pl.when(beside_me)
            def _():
                from_beside(s, c).wait_send()

            @pl.when(gy < last_y)
            def _():
                to_upper(s, c).wait_send()

    @pl.loop(0, chunks)
    def _(c):
        for k in range(4):
            @pl.when(reach[k][1])
            def _(k=k):
                edge_copy(k, c).wait_send()

        for k, present in enumerate((from_left, from_lower)):
            @pl.when(present)
            def _(k=k):
                early(k, c).wait_send()

    for k, present in enumerate((joins, joins_lower)):
        @pl.when(present)
        def _(k=k):
            lend(k).wait_send()


def flush(right, upper, residual, right_out, upper_out, residual_out, sem):
    copies = [
        pltpu.make_async_copy(right, right_out, sem.at[0]),
        pltpu.make_async_copy(upper, upper_out, sem.at[1]),
    ]
    for c in range(residual.shape[0]):
        lanes = pl.ds(c * LANES, LANES)
        copies.append(pltpu.make_async_copy(residual.at[c], residual_out.at[:, lanes], sem.at[2 + c]))
    for copy in copies:
        copy.start()
    for copy in copies:
        copy.wait()


def per_device(n_gx, n_gy, impedance, rebuild_map, left_trace, lower_trace, cell_kind, kind_wavenum):
    rows, sources = left_trace.shape[2:]
    cells = rebuild_map.shape[2]
    cx, cy = cell_kind.shape
    chunks = sources // LANES
    bf16, f32 = jnp.bfloat16, jnp.float32
    pair = lambda *shape: [pltpu.SemaphoreType.DMA(shape)] * 2
    right, upper, residual = pl.pallas_call(
        functools.partial(sweep, n_gx, n_gy),
        out_shape=(
            pltpu.VMEM((rows, sources), bf16),
            pltpu.VMEM((rows, sources), bf16),
            pltpu.VMEM((chunks, cells, LANES), f32),
        ),
        in_specs=[pl.BlockSpec(memory_space=pltpu.HBM)] * 6,
        out_specs=[pl.BlockSpec(memory_space=pltpu.VMEM)] * 3,
        scratch_shapes=[
            pltpu.VMEM((2 * rows, 2 * rows), bf16),
            pltpu.VMEM((cells, 2 * rows), bf16),
            pltpu.VMEM((STEPS, chunks, 2 * rows, LANES), bf16),
            pltpu.VMEM((STEPS - 1, chunks, 2 * rows, LANES), bf16),
            pltpu.VMEM((STEPS - 1, chunks, rows, LANES), bf16),
            pltpu.VMEM((4 * cy, 2 * rows), bf16),
            pltpu.VMEM((cells, LANES), f32),
            pltpu.VMEM((2, cells, LANES), f32),
            pltpu.VMEM((chunks, 4 * cy, LANES), bf16),
            pltpu.VMEM((chunks, 4 * cy, LANES), bf16),
            pltpu.VMEM((2, cy, rows), bf16),
            pltpu.VMEM((cy, 2 * rows), bf16),
            pltpu.VMEM((chunks, cy, LANES), bf16),
            pltpu.VMEM((2, chunks, cy, LANES), bf16),
            pltpu.VMEM((chunks, cy, LANES), bf16),
            pltpu.SMEM((cx, cy), jnp.int32),
            pltpu.SMEM(kind_wavenum.shape, f32),
            pltpu.SemaphoreType.DMA((2, chunks)),
            pltpu.SemaphoreType.DMA((7,)),
            *pair(STEPS - 1, chunks),
            *pair(STEPS - 1, chunks),
            *pair(STEPS - 1, chunks),
            *pair(4, chunks),
            *pair(2),
            pltpu.SemaphoreType.DMA((chunks,)),
            pltpu.SemaphoreType.DMA((2, chunks)),
        ],
        compiler_params=pltpu.CompilerParams(
            collective_id=0, has_side_effects=True, vmem_limit_bytes=40 * 2**20
        ),
        cost_estimate=pl.CostEstimate(flops=4_600_000_000, bytes_accessed=5_300_000, transcendentals=0),
        name="sweep",
    )(*[
        pltpu.with_memory_space_constraint(array, pltpu.HBM)
        for array in (impedance[0, 0], rebuild_map[0, 0], left_trace[0, 0], lower_trace[0, 0], cell_kind, kind_wavenum)
    ])
    right, upper, residual = pl.pallas_call(
        flush,
        out_shape=[jax.ShapeDtypeStruct((rows, sources), bf16)] * 2 + [jax.ShapeDtypeStruct((cells, sources), f32)],
        in_specs=[pl.BlockSpec(memory_space=pltpu.VMEM)] * 3,
        out_specs=[pl.BlockSpec(memory_space=pl.ANY)] * 3,
        scratch_shapes=[pltpu.SemaphoreType.DMA((2 + chunks,))],
        name="flush",
    )(*[pltpu.with_memory_space_constraint(array, pltpu.VMEM) for array in (right, upper, residual)])
    return right[None, None], upper[None, None], residual.reshape(cx, cy, sources)


def solution(mesh):
    return jax.shard_map(
        functools.partial(per_device, mesh.shape["gx"], mesh.shape["gy"]),
        mesh=mesh,
        in_specs=(
            P("gx", "gy", None, None),
            P("gx", "gy", None, None),
            P("gx", "gy", None, None),
            P("gx", "gy", None, None),
            P("gx", "gy"),
            P(),
        ),
        out_specs=(P("gx", "gy", None, None), P("gx", "gy", None, None), P("gx", "gy", None)),
        check_vma=False,
    )
```

```python
import functools

import jax
import jax.numpy as jnp
from jax import lax
from jax.experimental import pallas as pl
from jax.experimental.pallas import tpu as pltpu
from jax.sharding import PartitionSpec as P

MESH = pl.DeviceIdType.MESH
STEPS = 4
LANES = 128

def remote(src, dst, send_sem, recv_sem, device):
    return pltpu.make_async_remote_copy(
        src_ref=src, dst_ref=dst, send_sem=send_sem, recv_sem=recv_sem,
        device_id=device, device_id_type=MESH,
    )


def sweep(
    n_gx, n_gy,
    impedance, rebuild_map, left, lower, kinds_hbm, wavenum_hbm,
    right_out, upper_out, residual,
    amap, bmap, traces, outgoing, way, emap, factor, beside, edge_out, edge_in,
    lent, composed, early_out, early_in, joined,
    cell_kind, kind_wavenum, load_sem, map_sem, right_send, right_recv, upper_send, upper_recv, way_send, way_recv, edge_send, edge_recv,
    lend_send, lend_recv, early_send, early_recv,
):
    gx, gy = lax.axis_index("gx"), lax.axis_index("gy")
    rows = left.shape[0]
    chunks = left.shape[1] // LANES
    cells = rebuild_map.shape[0]
    cx, cy = cell_kind.shape
    half, last_x, last_y = n_gx // 2, n_gx - 1, n_gy - 1
    behind, ahead = lax.rem(gx + last_x, n_gx), lax.rem(gx + 1, n_gx)
    below, above = lax.rem(gy + last_y, n_gy), lax.rem(gy + 1, n_gy)

    quarter = rows // 2

    def map_load(k):
        part = pl.ds(k * quarter, quarter)
        return pltpu.make_async_copy(impedance.at[part, :], amap.at[part, :], map_sem.at[k])

    def rebuild_load():
        return pltpu.make_async_copy(rebuild_map, bmap, map_sem.at[6])

    def kinds_load():
        return pltpu.make_async_copy(kinds_hbm, cell_kind, map_sem.at[4])

    def wavenum_load():
        return pltpu.make_async_copy(wavenum_hbm, kind_wavenum, map_sem.at[5])

    def trace_load(side, c):
        source = (left, lower)[side]
        return pltpu.make_async_copy(
            source.at[:, pl.ds(c * LANES, LANES)], traces.at[0, c, pl.ds(side * rows, rows), :], load_sem.at[side, c]
        )

    for side in (0, 1):
        trace_load(side, 0).start()
    for k in range(4):
        map_load(k).start()
    for c in range(1, chunks):
        for side in (0, 1):
            trace_load(side, c).start()
    rebuild_load().start()
    kinds_load().start()
    wavenum_load().start()

    barrier = pltpu.get_barrier_semaphore()
    senders = (
        (gx > 0, (behind, gy)),
        (gy > 0, (gx, below)),
        (gx == last_x, (half - 1, gy)),
        (gx == half, (last_x, gy)),
        ((gx == half) & (lax.rem(gy, 2) == 0) & (gy > 0), (0, below)),
        ((gx == 0) & (lax.rem(gy, 2) == 0) & (gy > 0), (half, gy)),
    )
    for present, device in senders:
        @pl.when(present)
        def _(device=device):
            pl.semaphore_signal(barrier, inc=1, device_id=device, device_id_type=MESH)

    greeted = 0
    for present in (
        gx < last_x, gy < last_y, gx == half - 1, gx == last_x,
        (gx == 0) & (lax.rem(gy, 2) == 1) & (gy < last_y),
        (gx == half) & (lax.rem(gy, 2) == 0) & (gy > 0),
    ):
        greeted = greeted + jnp.where(present, 1, 0)

    def to_right(s, c):
        return remote(
            outgoing.at[s, c, pl.ds(0, rows), :], traces.at[s + 1, c, pl.ds(0, rows), :],
            right_send.at[s, c], right_recv.at[s, c], (ahead, gy),
        )

    def to_way(s, c):
        return remote(
            outgoing.at[s, c, pl.ds(0, rows), :], way.at[s, c], right_send.at[s, c], way_recv.at[s, c], (last_x, gy)
        )

    def from_way(s, c):
        return remote(
            way.at[s, c], traces.at[s + 1, c, pl.ds(0, rows), :], way_send.at[s, c], right_recv.at[s, c], (half, gy)
        )

    def to_upper(s, c):
        return remote(
            outgoing.at[s, c, pl.ds(rows, rows), :], traces.at[s + 1, c, pl.ds(rows, rows), :],
            upper_send.at[s, c], upper_recv.at[s, c], (gx, above),
        )

    def is_way(s, c):
        return ((s == 0) & (c >= chunks // 2))

    def send_right(s, c):
        by_way = (gx == half - 1) & is_way(s, c)

        @pl.when((gx < last_x) & jnp.logical_not(by_way))
        def _():
            to_right(s, c).start()

        @pl.when(by_way)
        def _():
            to_way(s, c).start()

    def arrived(s, c):
        @pl.when(gx > 0)
        def _():
            to_right(s, c).wait_recv()

        @pl.when(gy > 0)
        def _():
            to_upper(s, c).wait_recv()

    def relay(s, c):
        @pl.when((gx == last_x) & is_way(s, c))
        def _():
            to_way(s, c).wait_recv()
            from_way(s, c).start()

    odd = lax.rem(gy, 2) == 1
    detour = (gx == 0) & odd & (gy < last_y)
    beside_me = (gx == half) & jnp.logical_not(odd) & (gy > 0)

    def to_beside(s, c):
        return remote(
            outgoing.at[s, c, pl.ds(rows, rows), :], way.at[s, c], upper_send.at[s, c], way_recv.at[s, c], (half, above)
        )

    def from_beside(s, c):
        return remote(
            way.at[s, c], traces.at[s + 1, c, pl.ds(rows, rows), :], way_send.at[s, c], upper_recv.at[s, c], (0, gy)
        )

    def beside_relay(s, c):
        @pl.when(beside_me)
        def _():
            to_beside(s, c).wait_recv()
            from_beside(s, c).start()

    def multiply(s, c):
        return jnp.dot(amap[...], traces[s, c], preferred_element_type=jnp.float32).astype(jnp.bfloat16)

    def send_upper(s, c):
        @pl.when((gy < last_y) & jnp.logical_not(detour & (s > 0)))
        def _():
            to_upper(s, c).start()

        @pl.when(detour & (s > 0))
        def _():
            to_beside(s, c).start()

    def advance(s, c):
        outgoing[s, c] = multiply(s, c)
        send_right(s, c)
        send_upper(s, c)

    for side in (0, 1):
        trace_load(side, 0).wait()
    for k in range(4):
        map_load(k).wait()
        part = pl.ds(k * quarter, quarter)
        outgoing[0, 0, part, :] = jnp.dot(
            amap[part, :], traces[0, 0], preferred_element_type=jnp.float32
        ).astype(jnp.bfloat16)
        if k == 1:
            pl.semaphore_wait(barrier, greeted)
            send_right(0, 0)
    send_upper(0, 0)

    @pl.loop(1, chunks)
    def _(c):
        trace_load(0, c).wait()
        trace_load(1, c).wait()
        advance(0, c)

    def clear(side):
        @pl.loop(1, STEPS)
        def _(s):
            @pl.loop(0, chunks)
            def _(c):
                traces[s, c, pl.ds(side * rows, rows), :] = jnp.zeros((rows, LANES), traces.dtype)

    def clear_edge(k):
        edge_in[:, pl.ds(k * cy, cy), :] = jnp.zeros((chunks, cy, LANES), edge_in.dtype)

    @pl.when(gx == 0)
    def _():
        clear(0)
        clear_edge(0)

    @pl.when(gx == last_x)
    def _():
        clear_edge(1)

    @pl.when(gy == 0)
    def _():
        clear(1)
        clear_edge(2)

    @pl.when(gy == last_y)
    def _():
        clear_edge(3)

    rebuild_load().wait()
    row = lax.broadcasted_iota(jnp.int32, (4 * cy, cells), 0)
    side, along = lax.div(row, cy), lax.rem(row, cy)
    chosen = jnp.where(
        side == 0, cells - cy + along, jnp.where(side == 1, along, jnp.where(side == 2, along * cy + cy - 1, along * cy))
    )
    chosen = lax.broadcasted_iota(jnp.int32, (4 * cy, cells), 1) == chosen
    emap[...] = jnp.dot(
        jnp.where(chosen, 1.0, 0.0).astype(jnp.bfloat16), bmap[...], preferred_element_type=jnp.float32
    ).astype(jnp.bfloat16)

    from_left, from_lower = gx == half - 2, (gx == half - 1) & (gy < last_y)
    joins, joins_lower = gx == half - 1, (gx == half - 1) & (gy > 0)

    def lend(k):
        return remote(
            bmap.at[pl.ds(cells - cy, cy), pl.ds(k * rows, rows)], lent.at[k], lend_send.at[k], lend_recv.at[k],
            ((behind, gy), (gx, below))[k],
        )

    def early(k, c):
        return remote(
            early_out.at[c], early_in.at[k, c], early_send.at[c], early_recv.at[k, c], ((ahead, gy), (gx, above))[k]
        )

    def lend_rows():
        for k, present in enumerate((joins, joins_lower)):
            @pl.when(present)
            def _(k=k):
                lend(k).start()

    def compose():
        for k, present in enumerate((from_left, from_lower)):
            @pl.when(present)
            def _(k=k):
                lend(k).wait_recv()
                composed[...] = jnp.dot(
                    lent[k], amap[pl.ds(k * rows, rows), :], preferred_element_type=jnp.float32
                ).astype(composed.dtype)

    def send_early(c):
        @pl.when(from_left | from_lower)
        def _():
            early_out[c] = jnp.dot(
                composed[...], traces[STEPS - 2, c], preferred_element_type=jnp.float32
            ).astype(early_out.dtype)

        for k, present in enumerate((from_left, from_lower)):
            @pl.when(present)
            def _(k=k):
                early(k, c).start()

    def join_early(c):
        early(0, c).wait_recv()

        @pl.when(gy > 0)
        def _():
            early(1, c).wait_recv()

        joined[c] = (early_in[0, c].astype(jnp.float32) + early_in[1, c].astype(jnp.float32)).astype(joined.dtype)
        remote(
            joined.at[c], edge_in.at[c, pl.ds(0, cy), :], edge_send.at[0, c], edge_recv.at[0, c], (ahead, gy)
        ).start()

    @pl.when((gx == half - 1) & (gy == 0))
    def _():
        early_in[1] = jnp.zeros(early_in.shape[1:], early_in.dtype)

    @pl.loop(1, STEPS - 1)
    def _(s):
        @pl.loop(0, chunks)
        def _(c):
            arrived(s - 1, c)

            @pl.when((s == 1) & (c == 0))
            def _():
                lend_rows()

            @pl.when((s == 2) & (c == 0))
            def _():
                compose()

            @pl.when(s == 2)
            def _():
                send_early(c)

            advance(s, c)

            @pl.when((s == 1) & (c < chunks // 2))
            def _():
                relay(0, c + chunks // 2)

            beside_relay(s, c)

            @pl.when(joins & (s == STEPS - 2) & (c == chunks - 1))
            def _():
                @pl.loop(0, chunks - 1)
                def _(k):
                    join_early(k)


    reach = (
        (gx > 0, gx < last_x, (ahead, gy)),
        (gx < last_x, gx > 0, (behind, gy)),
        (gy > 0, gy < last_y, (gx, above)),
        (gy < last_y, gy > 0, (gx, below)),
    )

    def edge_copy(k, c):
        part = pl.ds(k * cy, cy)
        return remote(
            edge_out.at[c, part, :], edge_in.at[c, part, :], edge_send.at[k, c], edge_recv.at[k, c], reach[k][2]
        )

    def send_edges(c):
        edge_out[c] = jnp.dot(
            emap[...], traces[STEPS - 1, c], preferred_element_type=jnp.float32
        ).astype(edge_out.dtype)
        for k in range(4):
            @pl.when(reach[k][1] & jnp.logical_not(joins) if k == 0 else reach[k][1])
            def _(k=k):
                edge_copy(k, c).start()

    first, last = pl.ds(0, cx, stride=cy), pl.ds(cy - 1, cx, stride=cy)

    def rebuild(c):
        cell = jnp.dot(bmap[...], traces[STEPS - 1, c], preferred_element_type=jnp.float32)
        none = jnp.zeros((cy, LANES), jnp.float32)
        beside[0] = pltpu.roll(cell, 1, 0)
        beside[1] = pltpu.roll(cell, cells - 1, 0)
        beside[0, first, :] = none
        beside[1, last, :] = none
        along_x = jnp.concatenate([none, cell[: cells - cy]], axis=0) + jnp.concatenate([cell[cy:], none], axis=0)
        residual[c] = along_x + beside[0] + beside[1] + factor[...] * cell

    def finish(c):
        for k in range(4):
            @pl.when(reach[k][0])
            def _(k=k):
                edge_copy(k, c).wait_recv()
        for k, part in enumerate((pl.ds(0, cy), pl.ds(cells - cy, cy), first, last)):
            residual[c, part, :] += edge_in[c, pl.ds(k * cy, cy), :].astype(jnp.float32)

    @pl.loop(0, chunks)
    def _(c):
        arrived(STEPS - 2, c)
        send_edges(c)

        @pl.when(c == 0)
        def _():
            @pl.when(joins)
            def _():
                join_early(chunks - 1)

            kinds_load().wait()
            wavenum_load().wait()

            @pl.loop(0, cx)
            def _(a):
                for b in range(cy):
                    factor[pl.ds(a * cy + b, 1), :] = jnp.full(
                        (1, LANES), kind_wavenum[cell_kind[a, b]] - 4.0, jnp.float32
                    )

        rebuild(c)
        lanes = pl.ds(pl.multiple_of(c * LANES, LANES), LANES)
        leaving = multiply(STEPS - 1, c)
        right_out[:, lanes] = leaving[:rows]
        upper_out[:, lanes] = leaving[rows:]

    @pl.loop(0, chunks)
    def _(c):
        finish(c)

    @pl.loop(0, STEPS - 1)
    def _(s):
        @pl.loop(0, chunks)
        def _(c):
            @pl.when(gx < last_x)
            def _():
                to_right(s, c).wait_send()

            @pl.when((gx == last_x) & is_way(s, c))
            def _():
                from_way(s, c).wait_send()

            @pl.when(beside_me & (s > 0))
            def _():
                from_beside(s, c).wait_send()

            @pl.when(gy < last_y)
            def _():
                to_upper(s, c).wait_send()

    @pl.loop(0, chunks)
    def _(c):
        for k in range(4):
            @pl.when(reach[k][1])
            def _(k=k):
                edge_copy(k, c).wait_send()

        for k, present in enumerate((from_left, from_lower)):
            @pl.when(present)
            def _(k=k):
                early(k, c).wait_send()

    for k, present in enumerate((joins, joins_lower)):
        @pl.when(present)
        def _(k=k):
            lend(k).wait_send()


def flush(right, upper, residual, right_out, upper_out, residual_out, sem):
    copies = [
        pltpu.make_async_copy(right, right_out, sem.at[0]),
        pltpu.make_async_copy(upper, upper_out, sem.at[1]),
    ]
    for c in range(residual.shape[0]):
        lanes = pl.ds(c * LANES, LANES)
        copies.append(pltpu.make_async_copy(residual.at[c], residual_out.at[:, lanes], sem.at[2 + c]))
    for copy in copies:
        copy.start()
    for copy in copies:
        copy.wait()


def per_device(n_gx, n_gy, impedance, rebuild_map, left_trace, lower_trace, cell_kind, kind_wavenum):
    rows, sources = left_trace.shape[2:]
    cells = rebuild_map.shape[2]
    cx, cy = cell_kind.shape
    chunks = sources // LANES
    bf16, f32 = jnp.bfloat16, jnp.float32
    pair = lambda *shape: [pltpu.SemaphoreType.DMA(shape)] * 2
    right, upper, residual = pl.pallas_call(
        functools.partial(sweep, n_gx, n_gy),
        out_shape=(
            pltpu.VMEM((rows, sources), bf16),
            pltpu.VMEM((rows, sources), bf16),
            pltpu.VMEM((chunks, cells, LANES), f32),
        ),
        in_specs=[pl.BlockSpec(memory_space=pltpu.HBM)] * 6,
        out_specs=[pl.BlockSpec(memory_space=pltpu.VMEM)] * 3,
        scratch_shapes=[
            pltpu.VMEM((2 * rows, 2 * rows), bf16),
            pltpu.VMEM((cells, 2 * rows), bf16),
            pltpu.VMEM((STEPS, chunks, 2 * rows, LANES), bf16),
            pltpu.VMEM((STEPS - 1, chunks, 2 * rows, LANES), bf16),
            pltpu.VMEM((STEPS - 1, chunks, rows, LANES), bf16),
            pltpu.VMEM((4 * cy, 2 * rows), bf16),
            pltpu.VMEM((cells, LANES), f32),
            pltpu.VMEM((2, cells, LANES), f32),
            pltpu.VMEM((chunks, 4 * cy, LANES), bf16),
            pltpu.VMEM((chunks, 4 * cy, LANES), bf16),
            pltpu.VMEM((2, cy, rows), bf16),
            pltpu.VMEM((cy, 2 * rows), bf16),
            pltpu.VMEM((chunks, cy, LANES), bf16),
            pltpu.VMEM((2, chunks, cy, LANES), bf16),
            pltpu.VMEM((chunks, cy, LANES), bf16),
            pltpu.SMEM((cx, cy), jnp.int32),
            pltpu.SMEM(kind_wavenum.shape, f32),
            pltpu.SemaphoreType.DMA((2, chunks)),
            pltpu.SemaphoreType.DMA((7,)),
            *pair(STEPS - 1, chunks),
            *pair(STEPS - 1, chunks),
            *pair(STEPS - 1, chunks),
            *pair(4, chunks),
            *pair(2),
            pltpu.SemaphoreType.DMA((chunks,)),
            pltpu.SemaphoreType.DMA((2, chunks)),
        ],
        compiler_params=pltpu.CompilerParams(
            collective_id=0, has_side_effects=True, vmem_limit_bytes=40 * 2**20
        ),
        cost_estimate=pl.CostEstimate(flops=4_600_000_000, bytes_accessed=5_300_000, transcendentals=0),
        name="sweep",
    )(*[
        pltpu.with_memory_space_constraint(array, pltpu.HBM)
        for array in (impedance[0, 0], rebuild_map[0, 0], left_trace[0, 0], lower_trace[0, 0], cell_kind, kind_wavenum)
    ])
    right, upper, residual = pl.pallas_call(
        flush,
        out_shape=[jax.ShapeDtypeStruct((rows, sources), bf16)] * 2 + [jax.ShapeDtypeStruct((cells, sources), f32)],
        in_specs=[pl.BlockSpec(memory_space=pltpu.VMEM)] * 3,
        out_specs=[pl.BlockSpec(memory_space=pl.ANY)] * 3,
        scratch_shapes=[pltpu.SemaphoreType.DMA((2 + chunks,))],
        name="flush",
    )(*[pltpu.with_memory_space_constraint(array, pltpu.VMEM) for array in (right, upper, residual)])
    return right[None, None], upper[None, None], residual.reshape(cx, cy, sources)


def solution(mesh):
    return jax.shard_map(
        functools.partial(per_device, mesh.shape["gx"], mesh.shape["gy"]),
        mesh=mesh,
        in_specs=(
            P("gx", "gy", None, None),
            P("gx", "gy", None, None),
            P("gx", "gy", None, None),
            P("gx", "gy", None, None),
            P("gx", "gy"),
            P(),
        ),
        out_specs=(P("gx", "gy", None, None), P("gx", "gy", None, None), P("gx", "gy", None)),
        check_vma=False,
    )
```
